32 devices in a mesh: blk: 8 (over y, x, core), cast: 4 (over z).
Axes of the slice: x: 2, y: 2, z: 4, core: 2. Of those that a mesh axis runs over, the one named last changes fastest.
Arguments:
- film_temp: float32 [16, 128, 2048], P(None, 'cast', 'blk'), may hold values from -6 to 6
- surface_temp: float32 [128, 2048], P('cast', 'blk'), may hold values from 0.5 to 2
- shell_enthalpy: float32 [64, 128, 2048], P('blk', 'cast'), may hold values from 0 to 3
- phase_codes: int32 [16, 64], P('cast', 'blk'), may hold values from 0 to 2
- zone_ids: int32 [8], P('cast'), may hold values from 0 to 7
- zone_htc: float32 [8], replicated, may hold values from 0.5 to 1.5
Outputs:
- film_out: float32 [16, 128, 2048], P(None, 'cast', 'blk')
- shell_out: float32 [64, 128, 2048], P('blk', 'cast')
- surface_out: float32 [128, 2048], P('cast', 'blk')
The draws below stay inside these ranges and needn't reach their ends.
All inputs are finite; a program needn't handle non-finite values.
Results may differ from the reference program's by a relative error of at most 0.00002.
Values sent between devices are 32-bit elements; how exact they have to be, the bound alone decides.
A program may use at most 128 MiB of HBM per device.

```python
import math
import jax
import jax.numpy as jnp
from jax import lax

LAYERS = 16
TILE_R = 8
TILE_P = 32
ZONE_ROWS = 16
ZONES = 8
FILM_SWEEPS = 4
SHELL_SWEEPS = 10
PERIM = 2048
ROWS = 128
DEPTH = 64


def set_ends(drawn, stream_key, least, largest):
    dims = drawn.shape
    index_at = [jax.random.randint(jax.random.fold_in(stream_key, axis), (), 0, dims[axis]) for axis in range(len(dims))]
    drawn = drawn.at[tuple(index_at)].set(least)
    longest = dims.index(max(dims))
    index_at[longest] = (index_at[longest] + 1) % dims[longest]
    return drawn.at[tuple(index_at)].set(largest)


def shard_levels(key, extent, cuts, smallest, largest):
    def one(axis_at, blocks):
        draws = jax.random.uniform(jax.random.fold_in(jax.random.fold_in(key, 6), axis_at), (blocks,), jnp.float32, smallest / len(cuts), largest / len(cuts))
        return jnp.repeat(jnp.exp(draws), extent[axis_at] // blocks).reshape((-1,) + (1,) * (len(extent) - axis_at - 1))

    loudness = one(*cuts[0])
    for cut in cuts[1:]:
        loudness = loudness * one(*cut)
    return loudness


def centred(rng, shape, scale, reach, pieces=(), kind=jnp.bfloat16):
    entries = jax.random.normal(rng, shape, jnp.float32) * scale
    if len(pieces) > 0:
        entries = shard_levels(rng, shape, pieces, -0.22, 0.18) * entries
    return jnp.clip(entries, min=-reach, max=reach).astype(kind)


def setup_inputs(seed: int = 0) -> dict:
    streams_of = jax.random.split(jax.random.key(seed), 7)
    film_temp = centred(streams_of[0], (LAYERS, ROWS, PERIM), 1.0, 6.0, ((1, 4), (2, 8)), jnp.float32)
    surface_temp = jnp.clip(0.5 + 1.5 * jax.random.uniform(streams_of[1], (ROWS, PERIM), jnp.float32) ** shard_levels(streams_of[1], (ROWS, PERIM), ((0, 4), (1, 8)), -0.2, 0.2), 0.5, 2.0)
    shell_enthalpy = jnp.clip(3.0 * jax.random.uniform(streams_of[2], (DEPTH, ROWS, PERIM), jnp.float32) ** shard_levels(streams_of[2], (DEPTH, ROWS, PERIM), ((0, 8), (1, 4)), -0.2, 0.2), 0.0, 3.0)
    phase_codes = set_ends(jax.random.randint(streams_of[3], (ROWS // TILE_R, PERIM // TILE_P), 0, 3), jax.random.fold_in(streams_of[3], 1), 0, 2).astype(jnp.int32)
    zone_ids = set_ends(jax.random.randint(streams_of[4], (ROWS // ZONE_ROWS,), 0, ZONES), jax.random.fold_in(streams_of[4], 1), 0, ZONES - 1).astype(jnp.int32)
    zone_htc = jnp.clip(jnp.exp(jax.random.uniform(streams_of[5], (ZONES,), jnp.float32, math.log(0.5), math.log(1.5))), 0.5, 1.5)
    return dict(film_temp=film_temp, surface_temp=surface_temp, shell_enthalpy=shell_enthalpy, phase_codes=phase_codes, zone_ids=zone_ids, zone_htc=zone_htc)


normal_gain = 2.0
advance_flux_film = 0.1
shell_step = 0.15


def tile_conductivity(phase_codes):
    values = jnp.where(phase_codes == 0, 1.0, jnp.where(phase_codes == 1, 0.55, 0.3)).astype(jnp.float32)
    count_r, count_p = values.shape
    spread = jnp.broadcast_to(values[:, None, :, None], (count_r, TILE_R, count_p, TILE_P))
    return spread.reshape(count_r * TILE_R, count_p * TILE_P)


def row_cooling(zone_ids, zone_htc):
    onehot = (zone_ids[:, None] == jnp.arange(ZONES, dtype=jnp.int32)[None, :]).astype(zone_htc.dtype)
    per_block = jnp.sum(onehot * zone_htc[None, :], axis=1)
    return jnp.repeat(per_block, ZONE_ROWS)


def thermal_map(heat_content_per_mass):
    return jnp.minimum(heat_content_per_mass, 1.0) + jnp.maximum(heat_content_per_mass - 2.0, 0.0)


def film_update(film, sideways_conduction, conduct, cooling, crust_outer_face):
    below = jnp.concatenate([film[:1], film[:-1]], 0)
    above = jnp.concatenate([film[1:], crust_outer_face[None]], 0)
    normal = normal_gain * conduct * (above + below - 2.0 * film)
    normal = normal.at[0].add(-cooling[:, None] * film[0])
    return film + advance_flux_film * (conduct * sideways_conduction + normal)


def shell_sweep(heat_content_per_mass, flux):
    pointwise_heat_level = thermal_map(heat_content_per_mass)
    inner_neighbour = jnp.concatenate([pointwise_heat_level[1:], pointwise_heat_level[-1:]], 0)
    outer_neighbour = jnp.concatenate([pointwise_heat_level[:1], pointwise_heat_level[:-1]], 0)
    forward_neighbour = jnp.concatenate([pointwise_heat_level[:, 1:], pointwise_heat_level[:, -1:]], 1)
    trailing_neighbour = jnp.concatenate([pointwise_heat_level[:, :1], pointwise_heat_level[:, :-1]], 1)
    iteration_counter = inner_neighbour + outer_neighbour + forward_neighbour + trailing_neighbour + jnp.roll(pointwise_heat_level, 1, 2) + jnp.roll(pointwise_heat_level, -1, 2) - 6.0 * pointwise_heat_level
    heat_content_per_mass = heat_content_per_mass + shell_step * iteration_counter
    return heat_content_per_mass.at[0].add(shell_step * flux)


def reference(film_temp, surface_temp, shell_enthalpy, phase_codes, zone_ids, zone_htc):
    conduct = tile_conductivity(phase_codes)
    cooling = row_cooling(zone_ids, zone_htc)
    film = film_temp
    for sweep in range(FILM_SWEEPS):
        forward_neighbour = jnp.concatenate([film[:, 1:], film[:, -1:]], 1)
        trailing_neighbour = jnp.concatenate([film[:, :1], film[:, :-1]], 1)
        sideways_conduction = forward_neighbour + trailing_neighbour + jnp.roll(film, 1, 2) + jnp.roll(film, -1, 2) - 4.0 * film
        film = film_update(film, sideways_conduction, conduct, cooling, surface_temp)
    flux = normal_gain * conduct * (film[-1] - surface_temp)
    frozen_crust = lax.fori_loop(0, SHELL_SWEEPS, lambda step, state: shell_sweep(state, flux), shell_enthalpy)
    crust_outer_face = thermal_map(frozen_crust[0])
    return film, frozen_crust, crust_outer_face
```

```python
import functools

import jax
import jax.numpy as jnp
from jax import lax
from jax.experimental import pallas as pl
from jax.experimental.pallas import tpu as pltpu
from jax.sharding import PartitionSpec as P

TILE_R = 8
TILE_P = 32
ZONE_ROWS = 16
ZONES = 8
FILM_SWEEPS = 4
SHELL_SWEEPS = 10
W = FILM_SWEEPS

normal_gain = 2.0
advance_flux_film = 0.1
shell_step = 0.15


def thermal_map(h):
    return jnp.minimum(h, 1.0) + jnp.maximum(h - 2.0, 0.0)


def remote(src, dst, send_sem, recv_sem, device):
    return pltpu.make_async_remote_copy(
        src_ref=src,
        dst_ref=dst,
        send_sem=send_sem,
        recv_sem=recv_sem,
        device_id=device,
        device_id_type=pl.DeviceIdType.MESH,
    )


def kernel(
    n,
    m,
    film_ref,
    surf_ref,
    shell_ref,
    codes_ref,
    zone_ref,
    htc_ref,
    film_out,
    shell_out,
    surf_out,
    X,
    col_out,
    col_in,
    row_out,
    row_in,
    corner_out,
    corner_in,
    corner_all,
    U,
    edge_out,
    edge_in,
    heat,
    flux_out,
    face_in,
    film_send,
    film_recv,
    flux_send,
    flux_recv,
    face_send,
    face_recv,
    depth_send,
    depth_recv,
    edge_send,
    edge_recv,
):
    b = lax.axis_index("blk")
    z = lax.axis_index("cast")
    layers, rows, width = film_ref.shape
    depth, _, perim = shell_ref.shape
    tiles = rows // 8
    full = layers + 3
    left, right = lax.rem(b + n - 1, n), lax.rem(b + 1, n)
    has_up, has_down = z > 0, z < m - 1
    has_lo, has_hi = b > 0, b < n - 1

    barrier = pltpu.get_barrier_semaphore()
    for k in range(1, n):
        pl.semaphore_signal(
            barrier, inc=1, device_id={"blk": lax.rem(b + k, n)}, device_id_type=pl.DeviceIdType.MESH
        )

    @pl.when(has_up)
    def _():
        pl.semaphore_signal(barrier, inc=1, device_id={"cast": z - 1}, device_id_type=pl.DeviceIdType.MESH)

    @pl.when(has_down)
    def _():
        pl.semaphore_signal(barrier, inc=1, device_id={"cast": z + 1}, device_id_type=pl.DeviceIdType.MESH)

    lane = lax.broadcasted_iota(jnp.int32, (8, width), 1)
    X[0:layers, 0:rows, 0:width] = film_ref[...]
    X[layers, 0:rows, 0:width] = surf_ref[...]
    for i in range(tiles):
        values = jnp.zeros((8, width), jnp.float32)
        for j in range(width // TILE_P):
            code = codes_ref[i, j]
            value = jnp.where(code == 0, 1.0, jnp.where(code == 1, 0.55, 0.3)).astype(jnp.float32)
            values = jnp.where(lane // TILE_P == j, value, values)
        X[layers + 1, 8 * i : 8 * i + 8, 0:width] = values
    for i in range(rows // ZONE_ROWS):
        zone = zone_ref[i]
        htc = jnp.float32(0.0)
        for k in range(ZONES):
            htc = htc + jnp.where(zone == k, htc_ref[k], 0.0)
        X[layers + 2, ZONE_ROWS * i : ZONE_ROWS * (i + 1), 0:width] = jnp.full(
            (ZONE_ROWS, width), htc, jnp.float32
        )
    X[:, rows : rows + 8, :] = jnp.zeros((full, 8, width + 128), jnp.float32)

    lane_r = lax.broadcasted_iota(jnp.int32, (rows, 128), 1)
    first = jnp.zeros((rows, 128), jnp.float32)
    last = jnp.zeros((rows, 128), jnp.float32)
    for l in range(full):
        mine = (lane_r >= W * l) & (lane_r < W * (l + 1))
        first = jnp.where(mine, pltpu.roll(X[l, 0:rows, 0:128], W * l, axis=1), first)
        last = jnp.where(
            mine, pltpu.roll(X[l, 0:rows, width - 128 : width], (W * l + W) % 128, axis=1), last
        )
    col_out[0] = first
    col_out[1] = last
    row_out[0] = X[:, 0:W, 0:width]
    row_out[1] = X[:, rows - W : rows, 0:width]

    pl.semaphore_wait(barrier, n - 1 + jnp.where(has_up, 1, 0) + jnp.where(has_down, 1, 0))

    col_left = remote(col_out.at[0], col_in.at[1], film_send.at[0], film_recv.at[1], {"blk": left})
    col_right = remote(col_out.at[1], col_in.at[0], film_send.at[1], film_recv.at[0], {"blk": right})
    row_up = remote(row_out.at[0], row_in.at[1], film_send.at[2], film_recv.at[3], {"cast": z - 1})
    row_down = remote(row_out.at[1], row_in.at[0], film_send.at[3], film_recv.at[2], {"cast": z + 1})
    cor_up = remote(corner_out.at[0], corner_in.at[1], film_send.at[4], film_recv.at[5], {"cast": z - 1})
    cor_down = remote(corner_out.at[1], corner_in.at[0], film_send.at[5], film_recv.at[4], {"cast": z + 1})
    col_left.start()
    col_right.start()
    pl.when(has_up)(row_up.start)
    pl.when(has_down)(row_down.start)

    def lo_copy(p, r):
        part = pl.ds(8 * r, 8)
        return remote(
            U.at[p, 1, part], U.at[p, depth + 1, part], depth_send.at[p, 0, r], depth_recv.at[p, 1, r], {"blk": b - 1}
        )

    def hi_copy(p, r):
        part = pl.ds(8 * r, 8)
        return remote(
            U.at[p, depth, part], U.at[p, 0, part], depth_send.at[p, 1, r], depth_recv.at[p, 0, r], {"blk": b + 1}
        )

    def up_copy(p):
        return remote(edge_out.at[p, 0], edge_in.at[p, 1], edge_send.at[p, 0], edge_recv.at[p, 1], {"cast": z - 1})

    def down_copy(p):
        return remote(edge_out.at[p, 1], edge_in.at[p, 0], edge_send.at[p, 1], edge_recv.at[p, 0], {"cast": z + 1})

    def lo_arrives(p, r):
        hi_copy(p, r).wait_recv()

    def hi_arrives(p, r):
        lo_copy(p, r).wait_recv()

    def first_step(d, r):
        part = pl.ds(8 * r, 8)
        h = shell_ref[d, part, :]
        shell_out[d, part, :] = h
        u = thermal_map(h)
        U[0, d + 1, part, :] = u
        if r == 0:
            edge_out[0, 0, pl.ds(d, 1), :] = u[0:1, :]
        if r == tiles - 1:
            edge_out[0, 1, pl.ds(d, 1), :] = u[7:8, :]

    for r in range(tiles):
        first_step(0, r)
        pl.when(has_lo)(lo_copy(0, r).start)
        first_step(depth - 1, r)
        pl.when(has_hi)(hi_copy(0, r).start)

    @pl.loop(1, depth - 1)
    def _(d):
        for r in range(tiles):
            first_step(d, r)

    pl.when(has_up)(up_copy(0).start)
    pl.when(has_down)(down_copy(0).start)

    col_left.wait_recv()
    col_right.wait_recv()
    corner_out[0] = col_in[:, 0:W, :]
    corner_out[1] = col_in[:, rows - W : rows, :]
    pl.when(has_up)(cor_up.start)
    pl.when(has_down)(cor_down.start)

    def unpack(l, before, after, lanes):
        after = pltpu.roll(after, (128 - W * l) % 128, axis=1)
        before = pltpu.roll(before, 128 - W - W * l, axis=1)
        zero = jnp.zeros_like(after)
        return jnp.where(lanes < W, after, jnp.where(lanes >= 128 - W, before, zero))

    for l in range(full):
        X[l, 0:rows, width : width + 128] = unpack(l, col_in[0], col_in[1], lane_r)
    corner_all[...] = jnp.zeros_like(corner_all)

    @pl.when(has_up)
    def _():
        row_down.wait_recv()
        cor_down.wait_recv()
        X[:, rows + 8 - W : rows + 8, 0:width] = row_in[0]
        corner_all[:, 8 - W : 8, :] = corner_in[0]

    @pl.when(has_down)
    def _():
        row_up.wait_recv()
        cor_up.wait_recv()
        X[:, rows : rows + W, 0:width] = row_in[1]
        corner_all[:, 0:W, :] = corner_in[1]

    for l in range(full):
        X[l, rows : rows + 8, width : width + 128] = unpack(
            l, corner_all[0], corner_all[1], lane_r[0:8]
        )

    row_id = lax.broadcasted_iota(jnp.int32, (rows + 8, width + 128), 0)
    at_top = (row_id == 0) & (z == 0)
    at_bottom = (row_id == rows - 1) & (z == m - 1)
    conduct = layers + 1

    def film_layer(l, below, first):
        film = X[l]
        above = X[l + 1]
        k = X[conduct]
        prev_row = jnp.where(at_top, film, pltpu.roll(film, 1, axis=0))
        next_row = jnp.where(at_bottom, film, pltpu.roll(film, rows + 7, axis=0))
        lateral = (
            prev_row
            + next_row
            + pltpu.roll(film, 1, axis=1)
            + pltpu.roll(film, width + 127, axis=1)
            - 4.0 * film
        )
        normal = normal_gain * k * (above + below - 2.0 * film)
        if first:
            normal = normal - X[layers + 2] * film
        X[l] = film + advance_flux_film * (k * lateral + normal)
        return film

    @pl.loop(0, FILM_SWEEPS)
    def _(step):
        under = film_layer(0, X[0], True)
        lax.fori_loop(1, layers, lambda l, under: film_layer(l, under, False), under)

    flux = normal_gain * X[conduct, 0:rows, 0:width] * (
        X[layers - 1, 0:rows, 0:width] - X[layers, 0:rows, 0:width]
    )
    own = pl.ds(pl.multiple_of(b * width, width), width)
    to_root = remote(flux_out, heat.at[:, own], flux_send, flux_recv.at[b], {"blk": 0})

    @pl.when(has_lo)
    def _():
        flux_out[...] = flux
        to_root.start()
        heat[...] = jnp.zeros_like(heat)

    @pl.when(b == 0)
    def _():
        heat[:, 0:width] = flux

    film_out[...] = X[0:layers, 0:rows, 0:width]

    @pl.when(b == 0)
    def _():
        for k in range(1, n):
            remote(
                flux_out, heat.at[:, k * width : (k + 1) * width], flux_send, flux_recv.at[k], {"blk": 1}
            ).wait_recv()

    sub = lax.broadcasted_iota(jnp.int32, (8, perim), 0)

    def cell(p, q, d, r, below, above, heated, final):
        part = pl.ds(8 * r, 8)
        c = U[p, d + 1, part, :]
        if r == 0:
            edge = jnp.where(has_up, edge_in[p, 0, pl.ds(d, 1), :], c[0:1, :])
            prev_row = jnp.where(sub == 0, edge, pltpu.roll(c, 1, axis=0))
        else:
            prev_row = U[p, d + 1, pl.ds(8 * r - 1, 8), :]
        if r == tiles - 1:
            edge = jnp.where(has_down, edge_in[p, 1, pl.ds(d, 1), :], c[7:8, :])
            next_row = jnp.where(sub == 7, edge, pltpu.roll(c, 7, axis=0))
        else:
            next_row = U[p, d + 1, pl.ds(8 * r + 1, 8), :]
        lap = (
            U[p, below, part, :]
            + U[p, above, part, :]
            + prev_row
            + next_row
            + pltpu.roll(c, 1, axis=1)
            + pltpu.roll(c, perim - 1, axis=1)
            - 6.0 * c
        )
        h = shell_out[d, part, :] + shell_step * lap
        if heated:
            h = h + shell_step * heat[part, :]
        shell_out[d, part, :] = h
        if final and not heated:
            return
        u = thermal_map(h)
        U[q, d + 1, part, :] = u
        if final:
            return
        if r == 0:
            edge_out[q, 0, pl.ds(d, 1), :] = u[0:1, :]
        if r == tiles - 1:
            edge_out[q, 1, pl.ds(d, 1), :] = u[7:8, :]

    below_first = jnp.where(has_lo, 0, 1)
    above_last = jnp.where(has_hi, depth + 1, depth)

    def sweep(s, final):
        p = lax.rem(s, 2)
        q = 1 - p
        later = s >= 1
        pl.when(has_up & later)(lambda: up_copy(q).wait_send())
        pl.when(has_down & later)(lambda: down_copy(q).wait_send())
        pl.when(has_up)(lambda: down_copy(p).wait_recv())
        pl.when(has_down)(lambda: up_copy(p).wait_recv())
        for r in range(tiles):
            pl.when(has_lo & later)(lambda: lo_copy(q, r).wait_send())
            pl.when(has_lo)(lambda: lo_arrives(p, r))
            cell(p, q, 0, r, below_first, 2, True, final)
            if not final:
                pl.when(has_lo)(lambda: lo_copy(q, r).start())
            pl.when(has_hi & later)(lambda: hi_copy(q, r).wait_send())
            pl.when(has_hi)(lambda: hi_arrives(p, r))
            cell(p, q, depth - 1, r, depth - 1, above_last, False, final)
            if not final:
                pl.when(has_hi)(lambda: hi_copy(q, r).start())
        if final:

            @pl.when(b == 0)
            def _():
                for k in range(1, n):
                    face_copy(k).start()

        @pl.loop(1, depth - 1)
        def _(d):
            cell(p, q, d, 0, d, d + 2, False, final)
            cell(p, q, d, tiles - 1, d, d + 2, False, final)

        if not final:
            pl.when(has_up)(lambda: up_copy(q).start())
            pl.when(has_down)(lambda: down_copy(q).start())

        @pl.loop(1, depth - 1)
        def _(d):
            for r in range(1, tiles - 1):
                cell(p, q, d, r, d, d + 2, False, final)

    end = SHELL_SWEEPS % 2

    def face_copy(k):
        return remote(
            U.at[end, 1, :, k * width : (k + 1) * width], face_in, face_send.at[k], face_recv, {"blk": k}
        )

    @pl.loop(0, SHELL_SWEEPS - 1)
    def _(s):
        sweep(s, False)

    sweep(jnp.int32(SHELL_SWEEPS - 1), True)

    @pl.when(b == 0)
    def _():
        surf_out[...] = U[end, 1, :, 0:width]

    @pl.when(has_lo)
    def _():
        face_copy(1).wait_recv()
        surf_out[...] = face_in[...]

    @pl.when(b == 0)
    def _():
        for k in range(1, n):
            face_copy(k).wait_send()

    q = 1 - end
    col_left.wait_send()
    col_right.wait_send()

    @pl.when(has_up)
    def _():
        row_up.wait_send()
        cor_up.wait_send()
        up_copy(q).wait_send()

    @pl.when(has_down)
    def _():
        row_down.wait_send()
        cor_down.wait_send()
        down_copy(q).wait_send()

    @pl.when(has_lo)
    def _():
        to_root.wait_send()
        for r in range(tiles):
            lo_copy(q, r).wait_send()

    @pl.when(has_hi)
    def _():
        for r in range(tiles):
            hi_copy(q, r).wait_send()


def body(n, m, film_temp, surface_temp, shell_enthalpy, phase_codes, zone_ids, zone_htc):
    layers, rows, width = film_temp.shape
    depth, _, perim = shell_enthalpy.shape
    tiles = rows // 8
    full = layers + 3
    f32 = jnp.float32
    vmem = pl.BlockSpec(memory_space=pltpu.VMEM)
    smem = pl.BlockSpec(memory_space=pltpu.SMEM)
    dma = pltpu.SemaphoreType.DMA
    return pl.pallas_call(
        functools.partial(kernel, n, m),
        out_shape=[
            jax.ShapeDtypeStruct(film_temp.shape, f32),
            jax.ShapeDtypeStruct(shell_enthalpy.shape, f32),
            jax.ShapeDtypeStruct(surface_temp.shape, f32),
        ],
        in_specs=[vmem, vmem, vmem, smem, smem, smem],
        out_specs=[vmem, vmem, vmem],
        scratch_shapes=[
            pltpu.VMEM((full, rows + 8, width + 128), f32),
            pltpu.VMEM((2, rows, 128), f32),
            pltpu.VMEM((2, rows, 128), f32),
            pltpu.VMEM((2, full, W, width), f32),
            pltpu.VMEM((2, full, W, width), f32),
            pltpu.VMEM((2, 2, W, 128), f32),
            pltpu.VMEM((2, 2, W, 128), f32),
            pltpu.VMEM((2, 8, 128), f32),
            pltpu.VMEM((2, depth + 2, rows, perim), f32),
            pltpu.VMEM((2, 2, depth, perim), f32),
            pltpu.VMEM((2, 2, depth, perim), f32),
            pltpu.VMEM((rows, perim), f32),
            pltpu.VMEM((rows, width), f32),
            pltpu.VMEM((rows, width), f32),
            dma((6,)),
            dma((6,)),
            dma(()),
            dma((n,)),
            dma((n,)),
            dma(()),
            dma((2, 2, tiles)),
            dma((2, 2, tiles)),
            dma((2, 2)),
            dma((2, 2)),
        ],
        compiler_params=pltpu.CompilerParams(
            collective_id=0, has_side_effects=True, vmem_limit_bytes=48 * 1024 * 1024
        ),
    )(film_temp, surface_temp, shell_enthalpy, phase_codes, zone_ids, zone_htc)


def solution(mesh):
    placed = (
        P(None, "cast", "blk"),
        P("cast", "blk"),
        P("blk", "cast", None),
        P("cast", "blk"),
        P("cast"),
        P(),
    )
    return jax.shard_map(
        functools.partial(body, mesh.shape["blk"], mesh.shape["cast"]),
        mesh=mesh,
        in_specs=placed,
        out_specs=(P(None, "cast", "blk"), P("blk", "cast", None), P("cast", "blk")),
        check_vma=False,
    )
```

```python
import functools

import jax
import jax.numpy as jnp
from jax import lax
from jax.experimental import pallas as pl
from jax.experimental.pallas import tpu as pltpu
from jax.sharding import PartitionSpec as P

TILE_R = 8
TILE_P = 32
ZONE_ROWS = 16
ZONES = 8
FILM_SWEEPS = 4
SHELL_SWEEPS = 10
W = FILM_SWEEPS

normal_gain = 2.0
advance_flux_film = 0.1
shell_step = 0.15


def thermal_map(h):
    return jnp.minimum(h, 1.0) + jnp.maximum(h - 2.0, 0.0)


def remote(src, dst, send_sem, recv_sem, device):
    return pltpu.make_async_remote_copy(
        src_ref=src,
        dst_ref=dst,
        send_sem=send_sem,
        recv_sem=recv_sem,
        device_id=device,
        device_id_type=pl.DeviceIdType.MESH,
    )


def kernel(
    n,
    m,
    film_ref,
    surf_ref,
    shell_ref,
    codes_ref,
    zone_ref,
    htc_ref,
    film_out,
    shell_out,
    surf_out,
    X,
    col_out,
    col_in,
    row_out,
    row_in,
    corner_out,
    corner_in,
    corner_all,
    UA,
    UB,
    edge_out,
    edge_in,
    heat,
    flux_out,
    face_in,
    film_send,
    film_recv,
    flux_send,
    flux_recv,
    face_send,
    face_recv,
    depth_send,
    depth_recv,
    edge_send,
    edge_recv,
):
    U = (UA, UB)
    b = lax.axis_index("blk")
    z = lax.axis_index("cast")
    layers, rows, width = film_ref.shape
    depth, _, perim = shell_ref.shape
    tiles = rows // 8
    full = layers + 3
    left, right = lax.rem(b + n - 1, n), lax.rem(b + 1, n)
    has_up, has_down = z > 0, z < m - 1
    has_lo, has_hi = b > 0, b < n - 1

    barrier = pltpu.get_barrier_semaphore()
    for k in range(1, n):
        pl.semaphore_signal(
            barrier, inc=1, device_id={"blk": lax.rem(b + k, n)}, device_id_type=pl.DeviceIdType.MESH
        )

    @pl.when(has_up)
    def _():
        pl.semaphore_signal(barrier, inc=1, device_id={"cast": z - 1}, device_id_type=pl.DeviceIdType.MESH)

    @pl.when(has_down)
    def _():
        pl.semaphore_signal(barrier, inc=1, device_id={"cast": z + 1}, device_id_type=pl.DeviceIdType.MESH)

    lane = lax.broadcasted_iota(jnp.int32, (8, width), 1)
    X[0:layers, 0:rows, 0:width] = film_ref[...]
    X[layers, 0:rows, 0:width] = surf_ref[...]
    for i in range(tiles):
        values = jnp.zeros((8, width), jnp.float32)
        for j in range(width // TILE_P):
            code = codes_ref[i, j]
            value = jnp.where(code == 0, 1.0, jnp.where(code == 1, 0.55, 0.3)).astype(jnp.float32)
            values = jnp.where(lane // TILE_P == j, value, values)
        X[layers + 1, 8 * i : 8 * i + 8, 0:width] = values
    for i in range(rows // ZONE_ROWS):
        zone = zone_ref[i]
        htc = jnp.float32(0.0)
        for k in range(ZONES):
            htc = htc + jnp.where(zone == k, htc_ref[k], 0.0)
        X[layers + 2, ZONE_ROWS * i : ZONE_ROWS * (i + 1), 0:width] = jnp.full(
            (ZONE_ROWS, width), htc, jnp.float32
        )
    X[:, rows : rows + 8, :] = jnp.zeros((full, 8, width + 128), jnp.float32)

    lane_r = lax.broadcasted_iota(jnp.int32, (rows, 128), 1)
    first = jnp.zeros((rows, 128), jnp.float32)
    last = jnp.zeros((rows, 128), jnp.float32)
    for l in range(full):
        mine = (lane_r >= W * l) & (lane_r < W * (l + 1))
        first = jnp.where(mine, pltpu.roll(X[l, 0:rows, 0:128], W * l, axis=1), first)
        last = jnp.where(
            mine, pltpu.roll(X[l, 0:rows, width - 128 : width], (W * l + W) % 128, axis=1), last
        )
    col_out[0] = first
    col_out[1] = last
    row_out[0] = X[:, 0:W, 0:width]
    row_out[1] = X[:, rows - W : rows, 0:width]

    pl.semaphore_wait(barrier, n - 1 + jnp.where(has_up, 1, 0) + jnp.where(has_down, 1, 0))

    col_left = remote(col_out.at[0], col_in.at[1], film_send.at[0], film_recv.at[1], {"blk": left})
    col_right = remote(col_out.at[1], col_in.at[0], film_send.at[1], film_recv.at[0], {"blk": right})
    row_up = remote(row_out.at[0], row_in.at[1], film_send.at[2], film_recv.at[3], {"cast": z - 1})
    row_down = remote(row_out.at[1], row_in.at[0], film_send.at[3], film_recv.at[2], {"cast": z + 1})
    cor_up = remote(corner_out.at[0], corner_in.at[1], film_send.at[4], film_recv.at[5], {"cast": z - 1})
    cor_down = remote(corner_out.at[1], corner_in.at[0], film_send.at[5], film_recv.at[4], {"cast": z + 1})
    col_left.start()
    col_right.start()
    pl.when(has_up)(row_up.start)
    pl.when(has_down)(row_down.start)

    def lo_copy(p, r):
        part = pl.ds(8 * r, 8)
        return remote(
            U[p].at[1, part], U[p].at[depth + 1, part], depth_send.at[p, 0, r], depth_recv.at[p, 1, r], {"blk": b - 1}
        )

    def hi_copy(p, r):
        part = pl.ds(8 * r, 8)
        return remote(
            U[p].at[depth, part], U[p].at[0, part], depth_send.at[p, 1, r], depth_recv.at[p, 0, r], {"blk": b + 1}
        )

    def up_copy(p):
        return remote(edge_out.at[p, 0], edge_in.at[p, 1], edge_send.at[p, 0], edge_recv.at[p, 1], {"cast": z - 1})

    def down_copy(p):
        return remote(edge_out.at[p, 1], edge_in.at[p, 0], edge_send.at[p, 1], edge_recv.at[p, 0], {"cast": z + 1})

    def lo_arrives(p, r):
        hi_copy(p, r).wait_recv()

    def hi_arrives(p, r):
        lo_copy(p, r).wait_recv()

    def first_step(d, r):
        part = pl.ds(8 * r, 8)
        h = shell_ref[d, part, :]
        shell_out[d, part, :] = h
        u = thermal_map(h)
        UA[d + 1, part, :] = u
        if r == 0:
            edge_out[0, 0, pl.ds(d, 1), :] = u[0:1, :]
        if r == tiles - 1:
            edge_out[0, 1, pl.ds(d, 1), :] = u[7:8, :]

    for r in range(tiles):
        first_step(0, r)
        pl.when(has_lo)(lo_copy(0, r).start)
        first_step(depth - 1, r)
        pl.when(has_hi)(hi_copy(0, r).start)

    @pl.loop(1, depth - 1)
    def _(d):
        for r in range(tiles):
            first_step(d, r)

    pl.when(has_up)(up_copy(0).start)
    pl.when(has_down)(down_copy(0).start)

    col_left.wait_recv()
    col_right.wait_recv()
    corner_out[0] = col_in[:, 0:W, :]
    corner_out[1] = col_in[:, rows - W : rows, :]
    pl.when(has_up)(cor_up.start)
    pl.when(has_down)(cor_down.start)

    def unpack(l, before, after, lanes):
        after = pltpu.roll(after, (128 - W * l) % 128, axis=1)
        before = pltpu.roll(before, 128 - W - W * l, axis=1)
        zero = jnp.zeros_like(after)
        return jnp.where(lanes < W, after, jnp.where(lanes >= 128 - W, before, zero))

    for l in range(full):
        X[l, 0:rows, width : width + 128] = unpack(l, col_in[0], col_in[1], lane_r)
    corner_all[...] = jnp.zeros_like(corner_all)

    @pl.when(has_up)
    def _():
        row_down.wait_recv()
        cor_down.wait_recv()
        X[:, rows + 8 - W : rows + 8, 0:width] = row_in[0]
        corner_all[:, 8 - W : 8, :] = corner_in[0]

    @pl.when(has_down)
    def _():
        row_up.wait_recv()
        cor_up.wait_recv()
        X[:, rows : rows + W, 0:width] = row_in[1]
        corner_all[:, 0:W, :] = corner_in[1]

    for l in range(full):
        X[l, rows : rows + 8, width : width + 128] = unpack(
            l, corner_all[0], corner_all[1], lane_r[0:8]
        )

    row_id = lax.broadcasted_iota(jnp.int32, (rows + 8, width + 128), 0)
    at_top = (row_id == 0) & (z == 0)
    at_bottom = (row_id == rows - 1) & (z == m - 1)
    conduct = layers + 1

    def film_layer(l, below, first):
        film = X[l]
        above = X[l + 1]
        k = X[conduct]
        prev_row = jnp.where(at_top, film, pltpu.roll(film, 1, axis=0))
        next_row = jnp.where(at_bottom, film, pltpu.roll(film, rows + 7, axis=0))
        lateral = (
            prev_row
            + next_row
            + pltpu.roll(film, 1, axis=1)
            + pltpu.roll(film, width + 127, axis=1)
            - 4.0 * film
        )
        normal = normal_gain * k * (above + below - 2.0 * film)
        if first:
            normal = normal - X[layers + 2] * film
        X[l] = film + advance_flux_film * (k * lateral + normal)
        return film

    @pl.loop(0, FILM_SWEEPS)
    def _(step):
        under = film_layer(0, X[0], True)
        lax.fori_loop(1, layers, lambda l, under: film_layer(l, under, False), under)

    flux = normal_gain * X[conduct, 0:rows, 0:width] * (
        X[layers - 1, 0:rows, 0:width] - X[layers, 0:rows, 0:width]
    )
    own = pl.ds(pl.multiple_of(b * width, width), width)
    to_root = remote(flux_out, heat.at[:, own], flux_send, flux_recv.at[b], {"blk": 0})

    @pl.when(has_lo)
    def _():
        flux_out[...] = flux
        to_root.start()
        heat[...] = jnp.zeros_like(heat)

    @pl.when(b == 0)
    def _():
        heat[:, 0:width] = flux

    film_out[...] = X[0:layers, 0:rows, 0:width]

    @pl.when(b == 0)
    def _():
        for k in range(1, n):
            remote(
                flux_out, heat.at[:, k * width : (k + 1) * width], flux_send, flux_recv.at[k], {"blk": 1}
            ).wait_recv()

    sub = lax.broadcasted_iota(jnp.int32, (8, perim), 0)

    def cell(p, q, d, r, below, above, heated, final):
        part = pl.ds(8 * r, 8)
        c = U[p][d + 1, part, :]
        if r == 0:
            edge = jnp.where(has_up, edge_in[p, 0, pl.ds(d, 1), :], c[0:1, :])
            prev_row = jnp.where(sub == 0, edge, pltpu.roll(c, 1, axis=0))
        else:
            prev_row = U[p][d + 1, pl.ds(8 * r - 1, 8), :]
        if r == tiles - 1:
            edge = jnp.where(has_down, edge_in[p, 1, pl.ds(d, 1), :], c[7:8, :])
            next_row = jnp.where(sub == 7, edge, pltpu.roll(c, 7, axis=0))
        else:
            next_row = U[p][d + 1, pl.ds(8 * r + 1, 8), :]
        lap = (
            U[p][below, part, :]
            + U[p][above, part, :]
            + prev_row
            + next_row
            + pltpu.roll(c, 1, axis=1)
            + pltpu.roll(c, perim - 1, axis=1)
            - 6.0 * c
        )
        h = shell_out[d, part, :] + shell_step * lap
        if heated:
            h = h + shell_step * heat[part, :]
        shell_out[d, part, :] = h
        if final and not heated:
            return
        u = thermal_map(h)
        U[q][d + 1, part, :] = u
        if final:
            return
        if r == 0:
            edge_out[q, 0, pl.ds(d, 1), :] = u[0:1, :]
        if r == tiles - 1:
            edge_out[q, 1, pl.ds(d, 1), :] = u[7:8, :]

    below_first = jnp.where(has_lo, 0, 1)
    above_last = jnp.where(has_hi, depth + 1, depth)

    def ends(p, r, later, final):
        q = 1 - p
        pl.when(has_lo & later)(lambda: lo_copy(q, r).wait_send())
        pl.when(has_hi & later)(lambda: hi_copy(q, r).wait_send())
        pl.when(has_lo)(lambda: lo_arrives(p, r))
        pl.when(has_hi)(lambda: hi_arrives(p, r))
        cell(p, q, 0, r, below_first, 2, True, final)
        cell(p, q, depth - 1, r, depth - 1, above_last, False, final)
        if not final:
            pl.when(has_lo)(lambda: lo_copy(q, r).start())
            pl.when(has_hi)(lambda: hi_copy(q, r).start())

    def sweep(p, later, final):
        q = 1 - p
        outer, inner = (0, tiles - 1), range(1, tiles - 1)
        pl.when(has_up & later)(lambda: up_copy(q).wait_send())
        pl.when(has_down & later)(lambda: down_copy(q).wait_send())
        pl.when(has_up)(lambda: down_copy(p).wait_recv())
        pl.when(has_down)(lambda: up_copy(p).wait_recv())
        for r in outer:
            ends(p, r, later, final)

        @pl.loop(1, depth - 1)
        def _(d):
            for r in outer:
                cell(p, q, d, r, d, d + 2, False, final)

        if not final:
            pl.when(has_up)(lambda: up_copy(q).start())
            pl.when(has_down)(lambda: down_copy(q).start())
        for r in inner:
            ends(p, r, later, final)
        if final:

            @pl.when(b == 0)
            def _():
                for k in range(1, n):
                    face_copy(k).start()

        @pl.loop(1, depth - 1)
        def _(d):
            for r in inner:
                cell(p, q, d, r, d, d + 2, False, final)

    end = SHELL_SWEEPS % 2

    def face_copy(k):
        return remote(
            U[end].at[1, :, k * width : (k + 1) * width], face_in, face_send.at[k], face_recv, {"blk": k}
        )

    pairs = (SHELL_SWEEPS - 1) // 2

    @pl.loop(0, pairs)
    def _(k):
        sweep(0, k >= 1, False)
        sweep(1, k >= 0, False)

    for step in range(2 * pairs, SHELL_SWEEPS):
        sweep(step % 2, has_up | True, step == SHELL_SWEEPS - 1)

    @pl.when(b == 0)
    def _():
        surf_out[...] = U[end][1, :, 0:width]

    @pl.when(has_lo)
    def _():
        face_copy(1).wait_recv()
        surf_out[...] = face_in[...]

    @pl.when(b == 0)
    def _():
        for k in range(1, n):
            face_copy(k).wait_send()

    q = 1 - end
    col_left.wait_send()
    col_right.wait_send()

    @pl.when(has_up)
    def _():
        row_up.wait_send()
        cor_up.wait_send()
        up_copy(q).wait_send()

    @pl.when(has_down)
    def _():
        row_down.wait_send()
        cor_down.wait_send()
        down_copy(q).wait_send()

    @pl.when(has_lo)
    def _():
        to_root.wait_send()
        for r in range(tiles):
            lo_copy(q, r).wait_send()

    @pl.when(has_hi)
    def _():
        for r in range(tiles):
            hi_copy(q, r).wait_send()


def body(n, m, film_temp, surface_temp, shell_enthalpy, phase_codes, zone_ids, zone_htc):
    layers, rows, width = film_temp.shape
    depth, _, perim = shell_enthalpy.shape
    tiles = rows // 8
    full = layers + 3
    f32 = jnp.float32
    vmem = pl.BlockSpec(memory_space=pltpu.VMEM)
    smem = pl.BlockSpec(memory_space=pltpu.SMEM)
    dma = pltpu.SemaphoreType.DMA
    return pl.pallas_call(
        functools.partial(kernel, n, m),
        out_shape=[
            jax.ShapeDtypeStruct(film_temp.shape, f32),
            jax.ShapeDtypeStruct(shell_enthalpy.shape, f32),
            jax.ShapeDtypeStruct(surface_temp.shape, f32),
        ],
        in_specs=[vmem, vmem, vmem, smem, smem, smem],
        out_specs=[vmem, vmem, vmem],
        scratch_shapes=[
            pltpu.VMEM((full, rows + 8, width + 128), f32),
            pltpu.VMEM((2, rows, 128), f32),
            pltpu.VMEM((2, rows, 128), f32),
            pltpu.VMEM((2, full, W, width), f32),
            pltpu.VMEM((2, full, W, width), f32),
            pltpu.VMEM((2, 2, W, 128), f32),
            pltpu.VMEM((2, 2, W, 128), f32),
            pltpu.VMEM((2, 8, 128), f32),
            pltpu.VMEM((depth + 2, rows, perim), f32),
            pltpu.VMEM((depth + 2, rows, perim), f32),
            pltpu.VMEM((2, 2, depth, perim), f32),
            pltpu.VMEM((2, 2, depth, perim), f32),
            pltpu.VMEM((rows, perim), f32),
            pltpu.VMEM((rows, width), f32),
            pltpu.VMEM((rows, width), f32),
            dma((6,)),
            dma((6,)),
            dma(()),
            dma((n,)),
            dma((n,)),
            dma(()),
            dma((2, 2, tiles)),
            dma((2, 2, tiles)),
            dma((2, 2)),
            dma((2, 2)),
        ],
        compiler_params=pltpu.CompilerParams(
            collective_id=0, has_side_effects=True, vmem_limit_bytes=48 * 1024 * 1024
        ),
    )(film_temp, surface_temp, shell_enthalpy, phase_codes, zone_ids, zone_htc)


def solution(mesh):
    placed = (
        P(None, "cast", "blk"),
        P("cast", "blk"),
        P("blk", "cast", None),
        P("cast", "blk"),
        P("cast"),
        P(),
    )
    return jax.shard_map(
        functools.partial(body, mesh.shape["blk"], mesh.shape["cast"]),
        mesh=mesh,
        in_specs=placed,
        out_specs=(P(None, "cast", "blk"), P("blk", "cast", None), P("cast", "blk")),
        check_vma=False,
    )
```

```python
import functools

import jax
import jax.numpy as jnp
from jax import lax
from jax.experimental import pallas as pl
from jax.experimental.pallas import tpu as pltpu
from jax.sharding import PartitionSpec as P

TILE_R = 8
TILE_P = 32
ZONE_ROWS = 16
ZONES = 8
FILM_SWEEPS = 4
SHELL_SWEEPS = 10
W = FILM_SWEEPS

normal_gain = 2.0
advance_flux_film = 0.1
shell_step = 0.15


def thermal_map(h):
    return jnp.minimum(h, 1.0) + jnp.maximum(h - 2.0, 0.0)


def remote(src, dst, send_sem, recv_sem, device):
    return pltpu.make_async_remote_copy(
        src_ref=src,
        dst_ref=dst,
        send_sem=send_sem,
        recv_sem=recv_sem,
        device_id=device,
        device_id_type=pl.DeviceIdType.MESH,
    )


def kernel(
    n,
    m,
    film_ref,
    surf_ref,
    shell_ref,
    codes_ref,
    zone_ref,
    htc_ref,
    film_out,
    shell_out,
    surf_out,
    X,
    col_out,
    col_in,
    row_out,
    row_in,
    corner_out,
    corner_in,
    corner_all,
    UA,
    UB,
    edge_out,
    edge_in,
    heat,
    flux_out,
    face_in,
    film_send,
    film_recv,
    flux_send,
    flux_recv,
    face_send,
    face_recv,
    depth_send,
    depth_recv,
    edge_send,
    edge_recv,
):
    U = (UA, UB)
    b = lax.axis_index("blk")
    z = lax.axis_index("cast")
    layers, rows, width = film_ref.shape
    depth, _, perim = shell_ref.shape
    tiles = rows // 8
    full = layers + 3
    left, right = lax.rem(b + n - 1, n), lax.rem(b + 1, n)
    has_up, has_down = z > 0, z < m - 1
    has_lo, has_hi = b > 0, b < n - 1

    barrier = pltpu.get_barrier_semaphore()
    for k in range(1, n):
        pl.semaphore_signal(
            barrier, inc=1, device_id={"blk": lax.rem(b + k, n)}, device_id_type=pl.DeviceIdType.MESH
        )

    @pl.when(has_up)
    def _():
        pl.semaphore_signal(barrier, inc=1, device_id={"cast": z - 1}, device_id_type=pl.DeviceIdType.MESH)

    @pl.when(has_down)
    def _():
        pl.semaphore_signal(barrier, inc=1, device_id={"cast": z + 1}, device_id_type=pl.DeviceIdType.MESH)

    lane = lax.broadcasted_iota(jnp.int32, (8, width), 1)
    X[0:layers, 0:rows, 0:width] = film_ref[...]
    X[layers, 0:rows, 0:width] = surf_ref[...]
    for i in range(tiles):
        values = jnp.zeros((8, width), jnp.float32)
        for j in range(width // TILE_P):
            code = codes_ref[i, j]
            value = jnp.where(code == 0, 1.0, jnp.where(code == 1, 0.55, 0.3)).astype(jnp.float32)
            values = jnp.where(lane // TILE_P == j, value, values)
        X[layers + 1, 8 * i : 8 * i + 8, 0:width] = values
    for i in range(rows // ZONE_ROWS):
        zone = zone_ref[i]
        htc = jnp.float32(0.0)
        for k in range(ZONES):
            htc = htc + jnp.where(zone == k, htc_ref[k], 0.0)
        X[layers + 2, ZONE_ROWS * i : ZONE_ROWS * (i + 1), 0:width] = jnp.full(
            (ZONE_ROWS, width), htc, jnp.float32
        )
    X[:, rows : rows + 8, :] = jnp.zeros((full, 8, width + 128), jnp.float32)

    lane_r = lax.broadcasted_iota(jnp.int32, (rows, 128), 1)
    first = jnp.zeros((rows, 128), jnp.float32)
    last = jnp.zeros((rows, 128), jnp.float32)
    for l in range(full):
        mine = (lane_r >= W * l) & (lane_r < W * (l + 1))
        first = jnp.where(mine, pltpu.roll(X[l, 0:rows, 0:128], W * l, axis=1), first)
        last = jnp.where(
            mine, pltpu.roll(X[l, 0:rows, width - 128 : width], (W * l + W) % 128, axis=1), last
        )
    col_out[0] = first
    col_out[1] = last
    row_out[0] = X[:, 0:W, 0:width]
    row_out[1] = X[:, rows - W : rows, 0:width]

    pl.semaphore_wait(barrier, n - 1 + jnp.where(has_up, 1, 0) + jnp.where(has_down, 1, 0))

    col_left = remote(col_out.at[0], col_in.at[1], film_send.at[0], film_recv.at[1], {"blk": left})
    col_right = remote(col_out.at[1], col_in.at[0], film_send.at[1], film_recv.at[0], {"blk": right})
    row_up = remote(row_out.at[0], row_in.at[1], film_send.at[2], film_recv.at[3], {"cast": z - 1})
    row_down = remote(row_out.at[1], row_in.at[0], film_send.at[3], film_recv.at[2], {"cast": z + 1})
    cor_up = remote(corner_out.at[0], corner_in.at[1], film_send.at[4], film_recv.at[5], {"cast": z - 1})
    cor_down = remote(corner_out.at[1], corner_in.at[0], film_send.at[5], film_recv.at[4], {"cast": z + 1})
    col_left.start()
    col_right.start()
    pl.when(has_up)(row_up.start)
    pl.when(has_down)(row_down.start)

    def lo_copy(p, r):
        part = pl.ds(8 * r, 8)
        return remote(
            U[p].at[1, part], U[p].at[depth + 1, part], depth_send.at[p, 0, r], depth_recv.at[p, 1, r], {"blk": b - 1}
        )

    def hi_copy(p, r):
        part = pl.ds(8 * r, 8)
        return remote(
            U[p].at[depth, part], U[p].at[0, part], depth_send.at[p, 1, r], depth_recv.at[p, 0, r], {"blk": b + 1}
        )

    def up_copy(p):
        return remote(edge_out.at[p, 0], edge_in.at[p, 1], edge_send.at[p, 0], edge_recv.at[p, 1], {"cast": z - 1})

    def down_copy(p):
        return remote(edge_out.at[p, 1], edge_in.at[p, 0], edge_send.at[p, 1], edge_recv.at[p, 0], {"cast": z + 1})

    def lo_arrives(p, r):
        hi_copy(p, r).wait_recv()

    def hi_arrives(p, r):
        lo_copy(p, r).wait_recv()

    def first_step(d, r):
        part = pl.ds(8 * r, 8)
        h = shell_ref[d, part, :]
        shell_out[d, part, :] = h
        u = thermal_map(h)
        UA[d + 1, part, :] = u
        if r == 0:
            edge_out[0, 0, pl.ds(d, 1), :] = u[0:1, :]
        if r == tiles - 1:
            edge_out[0, 1, pl.ds(d, 1), :] = u[7:8, :]

    for r in range(tiles):
        first_step(0, r)
        pl.when(has_lo)(lo_copy(0, r).start)
        first_step(depth - 1, r)
        pl.when(has_hi)(hi_copy(0, r).start)

    @pl.loop(1, depth - 1)
    def _(d):
        for r in range(tiles):
            first_step(d, r)

    pl.when(has_up)(up_copy(0).start)
    pl.when(has_down)(down_copy(0).start)

    col_left.wait_recv()
    col_right.wait_recv()
    corner_out[0] = col_in[:, 0:W, :]
    corner_out[1] = col_in[:, rows - W : rows, :]
    pl.when(has_up)(cor_up.start)
    pl.when(has_down)(cor_down.start)

    def unpack(l, before, after, lanes):
        after = pltpu.roll(after, (128 - W * l) % 128, axis=1)
        before = pltpu.roll(before, 128 - W - W * l, axis=1)
        zero = jnp.zeros_like(after)
        return jnp.where(lanes < W, after, jnp.where(lanes >= 128 - W, before, zero))

    for l in range(full):
        X[l, 0:rows, width : width + 128] = unpack(l, col_in[0], col_in[1], lane_r)
    corner_all[...] = jnp.zeros_like(corner_all)

    @pl.when(has_up)
    def _():
        row_down.wait_recv()
        cor_down.wait_recv()
        X[:, rows + 8 - W : rows + 8, 0:width] = row_in[0]
        corner_all[:, 8 - W : 8, :] = corner_in[0]

    @pl.when(has_down)
    def _():
        row_up.wait_recv()
        cor_up.wait_recv()
        X[:, rows : rows + W, 0:width] = row_in[1]
        corner_all[:, 0:W, :] = corner_in[1]

    for l in range(full):
        X[l, rows : rows + 8, width : width + 128] = unpack(
            l, corner_all[0], corner_all[1], lane_r[0:8]
        )

    row_id = lax.broadcasted_iota(jnp.int32, (rows + 8, width + 128), 0)
    at_top = (row_id == 0) & (z == 0)
    at_bottom = (row_id == rows - 1) & (z == m - 1)
    conduct = layers + 1

    def film_layer(l, below, first):
        film = X[l]
        above = X[l + 1]
        k = X[conduct]
        prev_row = jnp.where(at_top, film, pltpu.roll(film, 1, axis=0))
        next_row = jnp.where(at_bottom, film, pltpu.roll(film, rows + 7, axis=0))
        lateral = (
            prev_row
            + next_row
            + pltpu.roll(film, 1, axis=1)
            + pltpu.roll(film, width + 127, axis=1)
            - 4.0 * film
        )
        normal = normal_gain * k * (above + below - 2.0 * film)
        if first:
            normal = normal - X[layers + 2] * film
        X[l] = film + advance_flux_film * (k * lateral + normal)
        return film

    @pl.loop(0, FILM_SWEEPS)
    def _(step):
        under = film_layer(0, X[0], True)
        for l in range(1, layers):
            under = film_layer(l, under, False)

    flux = normal_gain * X[conduct, 0:rows, 0:width] * (
        X[layers - 1, 0:rows, 0:width] - X[layers, 0:rows, 0:width]
    )
    own = pl.ds(pl.multiple_of(b * width, width), width)
    to_root = remote(flux_out, heat.at[:, own], flux_send, flux_recv.at[b], {"blk": 0})

    @pl.when(has_lo)
    def _():
        flux_out[...] = flux
        to_root.start()
        heat[...] = jnp.zeros_like(heat)

    @pl.when(b == 0)
    def _():
        heat[:, 0:width] = flux

    film_out[...] = X[0:layers, 0:rows, 0:width]

    @pl.when(b == 0)
    def _():
        for k in range(1, n):
            remote(
                flux_out, heat.at[:, k * width : (k + 1) * width], flux_send, flux_recv.at[k], {"blk": 1}
            ).wait_recv()

    sub = lax.broadcasted_iota(jnp.int32, (8, perim), 0)

    def cell(p, q, d, r, below, above, heated, final):
        part = pl.ds(8 * r, 8)
        c = U[p][d + 1, part, :]
        if r == 0:
            edge = jnp.where(has_up, edge_in[p, 0, pl.ds(d, 1), :], c[0:1, :])
            prev_row = jnp.where(sub == 0, edge, pltpu.roll(c, 1, axis=0))
        else:
            prev_row = U[p][d + 1, pl.ds(8 * r - 1, 8), :]
        if r == tiles - 1:
            edge = jnp.where(has_down, edge_in[p, 1, pl.ds(d, 1), :], c[7:8, :])
            next_row = jnp.where(sub == 7, edge, pltpu.roll(c, 7, axis=0))
        else:
            next_row = U[p][d + 1, pl.ds(8 * r + 1, 8), :]
        lap = (
            U[p][below, part, :]
            + U[p][above, part, :]
            + prev_row
            + next_row
            + pltpu.roll(c, 1, axis=1)
            + pltpu.roll(c, perim - 1, axis=1)
            - 6.0 * c
        )
        h = shell_out[d, part, :] + shell_step * lap
        if heated:
            h = h + shell_step * heat[part, :]
        shell_out[d, part, :] = h
        if final and not heated:
            return
        u = thermal_map(h)
        U[q][d + 1, part, :] = u
        if final:
            return
        if r == 0:
            edge_out[q, 0, pl.ds(d, 1), :] = u[0:1, :]
        if r == tiles - 1:
            edge_out[q, 1, pl.ds(d, 1), :] = u[7:8, :]

    below_first = jnp.where(has_lo, 0, 1)
    above_last = jnp.where(has_hi, depth + 1, depth)

    def ends(p, r, later, final):
        q = 1 - p
        pl.when(has_lo & later)(lambda: lo_copy(q, r).wait_send())
        pl.when(has_hi & later)(lambda: hi_copy(q, r).wait_send())
        pl.when(has_lo)(lambda: lo_arrives(p, r))
        pl.when(has_hi)(lambda: hi_arrives(p, r))
        cell(p, q, 0, r, below_first, 2, True, final)
        cell(p, q, depth - 1, r, depth - 1, above_last, False, final)
        if not final:
            pl.when(has_lo)(lambda: lo_copy(q, r).start())
            pl.when(has_hi)(lambda: hi_copy(q, r).start())

    def sweep(p, later, final):
        q = 1 - p
        outer, inner = (0, tiles - 1), range(1, tiles - 1)
        pl.when(has_up & later)(lambda: up_copy(q).wait_send())
        pl.when(has_down & later)(lambda: down_copy(q).wait_send())
        pl.when(has_up)(lambda: down_copy(p).wait_recv())
        pl.when(has_down)(lambda: up_copy(p).wait_recv())
        for r in outer:
            ends(p, r, later, final)

        @pl.loop(1, depth - 1)
        def _(d):
            for r in outer:
                cell(p, q, d, r, d, d + 2, False, final)

        if not final:
            pl.when(has_up)(lambda: up_copy(q).start())
            pl.when(has_down)(lambda: down_copy(q).start())
        for r in inner:
            ends(p, r, later, final)
        if final:

            @pl.when(b == 0)
            def _():
                for k in range(1, n):
                    face_copy(k).start()

        @pl.loop(1, depth - 1)
        def _(d):
            for r in inner:
                cell(p, q, d, r, d, d + 2, False, final)

    end = SHELL_SWEEPS % 2

    def face_copy(k):
        return remote(
            U[end].at[1, :, k * width : (k + 1) * width], face_in, face_send.at[k], face_recv, {"blk": k}
        )

    pairs = (SHELL_SWEEPS - 1) // 2

    @pl.loop(0, pairs)
    def _(k):
        sweep(0, k >= 1, False)
        sweep(1, k >= 0, False)

    for step in range(2 * pairs, SHELL_SWEEPS):
        sweep(step % 2, has_up | True, step == SHELL_SWEEPS - 1)

    @pl.when(b == 0)
    def _():
        surf_out[...] = U[end][1, :, 0:width]

    @pl.when(has_lo)
    def _():
        face_copy(1).wait_recv()
        surf_out[...] = face_in[...]

    @pl.when(b == 0)
    def _():
        for k in range(1, n):
            face_copy(k).wait_send()

    q = 1 - end
    col_left.wait_send()
    col_right.wait_send()

    @pl.when(has_up)
    def _():
        row_up.wait_send()
        cor_up.wait_send()
        up_copy(q).wait_send()

    @pl.when(has_down)
    def _():
        row_down.wait_send()
        cor_down.wait_send()
        down_copy(q).wait_send()

    @pl.when(has_lo)
    def _():
        to_root.wait_send()
        for r in range(tiles):
            lo_copy(q, r).wait_send()

    @pl.when(has_hi)
    def _():
        for r in range(tiles):
            hi_copy(q, r).wait_send()


def body(n, m, film_temp, surface_temp, shell_enthalpy, phase_codes, zone_ids, zone_htc):
    layers, rows, width = film_temp.shape
    depth, _, perim = shell_enthalpy.shape
    tiles = rows // 8
    full = layers + 3
    f32 = jnp.float32
    vmem = pl.BlockSpec(memory_space=pltpu.VMEM)
    smem = pl.BlockSpec(memory_space=pltpu.SMEM)
    dma = pltpu.SemaphoreType.DMA
    return pl.pallas_call(
        functools.partial(kernel, n, m),
        out_shape=[
            jax.ShapeDtypeStruct(film_temp.shape, f32),
            jax.ShapeDtypeStruct(shell_enthalpy.shape, f32),
            jax.ShapeDtypeStruct(surface_temp.shape, f32),
        ],
        in_specs=[vmem, vmem, vmem, smem, smem, smem],
        out_specs=[vmem, vmem, vmem],
        scratch_shapes=[
            pltpu.VMEM((full, rows + 8, width + 128), f32),
            pltpu.VMEM((2, rows, 128), f32),
            pltpu.VMEM((2, rows, 128), f32),
            pltpu.VMEM((2, full, W, width), f32),
            pltpu.VMEM((2, full, W, width), f32),
            pltpu.VMEM((2, 2, W, 128), f32),
            pltpu.VMEM((2, 2, W, 128), f32),
            pltpu.VMEM((2, 8, 128), f32),
            pltpu.VMEM((depth + 2, rows, perim), f32),
            pltpu.VMEM((depth + 2, rows, perim), f32),
            pltpu.VMEM((2, 2, depth, perim), f32),
            pltpu.VMEM((2, 2, depth, perim), f32),
            pltpu.VMEM((rows, perim), f32),
            pltpu.VMEM((rows, width), f32),
            pltpu.VMEM((rows, width), f32),
            dma((6,)),
            dma((6,)),
            dma(()),
            dma((n,)),
            dma((n,)),
            dma(()),
            dma((2, 2, tiles)),
            dma((2, 2, tiles)),
            dma((2, 2)),
            dma((2, 2)),
        ],
        compiler_params=pltpu.CompilerParams(
            collective_id=0, has_side_effects=True, vmem_limit_bytes=48 * 1024 * 1024
        ),
    )(film_temp, surface_temp, shell_enthalpy, phase_codes, zone_ids, zone_htc)


def solution(mesh):
    placed = (
        P(None, "cast", "blk"),
        P("cast", "blk"),
        P("blk", "cast", None),
        P("cast", "blk"),
        P("cast"),
        P(),
    )
    return jax.shard_map(
        functools.partial(body, mesh.shape["blk"], mesh.shape["cast"]),
        mesh=mesh,
        in_specs=placed,
        out_specs=(P(None, "cast", "blk"), P("blk", "cast", None), P("cast", "blk")),
        check_vma=False,
    )
```

```python
import functools

import jax
import jax.numpy as jnp
from jax import lax
from jax.experimental import pallas as pl
from jax.experimental.pallas import tpu as pltpu
from jax.sharding import PartitionSpec as P

TILE_R = 8
TILE_P = 32
ZONE_ROWS = 16
ZONES = 8
FILM_SWEEPS = 4
SHELL_SWEEPS = 10
W = FILM_SWEEPS

normal_gain = 2.0
advance_flux_film = 0.1
shell_step = 0.15


def thermal_map(h):
    return jnp.minimum(h, 1.0) + jnp.maximum(h - 2.0, 0.0)


def remote(src, dst, send_sem, recv_sem, device):
    return pltpu.make_async_remote_copy(
        src_ref=src,
        dst_ref=dst,
        send_sem=send_sem,
        recv_sem=recv_sem,
        device_id=device,
        device_id_type=pl.DeviceIdType.MESH,
    )


def kernel(
    n,
    m,
    film_ref,
    surf_ref,
    shell_ref,
    codes_ref,
    zone_ref,
    htc_ref,
    film_out,
    shell_out,
    surf_out,
    X,
    col_out,
    col_in,
    row_out,
    row_in,
    corner_out,
    corner_in,
    corner_all,
    UA,
    UB,
    edge_out,
    edge_in,
    heat,
    flux_out,
    face_in,
    film_send,
    film_recv,
    flux_send,
    flux_recv,
    face_send,
    face_recv,
    depth_send,
    depth_recv,
    edge_send,
    edge_recv,
    load_sem,
):
    U = (UA, UB)
    b = lax.axis_index("blk")
    z = lax.axis_index("cast")
    layers, rows, width = film_ref.shape
    depth, _, perim = shell_ref.shape
    tiles = rows // 8
    full = layers + 3
    left, right = lax.rem(b + n - 1, n), lax.rem(b + 1, n)
    has_up, has_down = z > 0, z < m - 1
    has_lo, has_hi = b > 0, b < n - 1

    loads = (
        pltpu.make_async_copy(film_ref, X.at[0:layers, 0:rows, 0:width], load_sem.at[0]),
        pltpu.make_async_copy(surf_ref, X.at[layers, 0:rows, 0:width], load_sem.at[1]),
        pltpu.make_async_copy(shell_ref, shell_out, load_sem.at[2]),
    )
    for load in loads:
        load.start()

    barrier = pltpu.get_barrier_semaphore()
    for k in range(1, n):
        pl.semaphore_signal(
            barrier, inc=1, device_id={"blk": lax.rem(b + k, n)}, device_id_type=pl.DeviceIdType.MESH
        )

    @pl.when(has_up)
    def _():
        pl.semaphore_signal(barrier, inc=1, device_id={"cast": z - 1}, device_id_type=pl.DeviceIdType.MESH)

    @pl.when(has_down)
    def _():
        pl.semaphore_signal(barrier, inc=1, device_id={"cast": z + 1}, device_id_type=pl.DeviceIdType.MESH)

    lane = lax.broadcasted_iota(jnp.int32, (8, width), 1)
    for i in range(tiles):
        values = jnp.zeros((8, width), jnp.float32)
        for j in range(width // TILE_P):
            code = codes_ref[i, j]
            value = jnp.where(code == 0, 1.0, jnp.where(code == 1, 0.55, 0.3)).astype(jnp.float32)
            values = jnp.where(lane // TILE_P == j, value, values)
        X[layers + 1, 8 * i : 8 * i + 8, 0:width] = values
    for i in range(rows // ZONE_ROWS):
        zone = zone_ref[i]
        htc = jnp.float32(0.0)
        for k in range(ZONES):
            htc = htc + jnp.where(zone == k, htc_ref[k], 0.0)
        X[layers + 2, ZONE_ROWS * i : ZONE_ROWS * (i + 1), 0:width] = jnp.full(
            (ZONE_ROWS, width), htc, jnp.float32
        )
    X[:, rows : rows + 8, :] = jnp.zeros((full, 8, width + 128), jnp.float32)

    loads[0].wait()
    loads[1].wait()
    lane_r = lax.broadcasted_iota(jnp.int32, (rows, 128), 1)
    first = jnp.zeros((rows, 128), jnp.float32)
    last = jnp.zeros((rows, 128), jnp.float32)
    for l in range(full):
        mine = (lane_r >= W * l) & (lane_r < W * (l + 1))
        first = jnp.where(mine, pltpu.roll(X[l, 0:rows, 0:128], W * l, axis=1), first)
        last = jnp.where(
            mine, pltpu.roll(X[l, 0:rows, width - 128 : width], (W * l + W) % 128, axis=1), last
        )
    col_out[0] = first
    col_out[1] = last
    row_out[0] = X[:, 0:W, 0:width]
    row_out[1] = X[:, rows - W : rows, 0:width]

    pl.semaphore_wait(barrier, n - 1 + jnp.where(has_up, 1, 0) + jnp.where(has_down, 1, 0))

    col_left = remote(col_out.at[0], col_in.at[1], film_send.at[0], film_recv.at[1], {"blk": left})
    col_right = remote(col_out.at[1], col_in.at[0], film_send.at[1], film_recv.at[0], {"blk": right})
    row_up = remote(row_out.at[0], row_in.at[1], film_send.at[2], film_recv.at[3], {"cast": z - 1})
    row_down = remote(row_out.at[1], row_in.at[0], film_send.at[3], film_recv.at[2], {"cast": z + 1})
    cor_up = remote(corner_out.at[0], corner_in.at[1], film_send.at[4], film_recv.at[5], {"cast": z - 1})
    cor_down = remote(corner_out.at[1], corner_in.at[0], film_send.at[5], film_recv.at[4], {"cast": z + 1})
    col_left.start()
    col_right.start()
    pl.when(has_up)(row_up.start)
    pl.when(has_down)(row_down.start)

    def lo_copy(p, r):
        part = pl.ds(8 * r, 8)
        return remote(
            U[p].at[1, part], U[p].at[depth + 1, part], depth_send.at[p, 0, r], depth_recv.at[p, 1, r], {"blk": b - 1}
        )

    def hi_copy(p, r):
        part = pl.ds(8 * r, 8)
        return remote(
            U[p].at[depth, part], U[p].at[0, part], depth_send.at[p, 1, r], depth_recv.at[p, 0, r], {"blk": b + 1}
        )

    def up_copy(p):
        return remote(edge_out.at[p, 0], edge_in.at[p, 1], edge_send.at[p, 0], edge_recv.at[p, 1], {"cast": z - 1})

    def down_copy(p):
        return remote(edge_out.at[p, 1], edge_in.at[p, 0], edge_send.at[p, 1], edge_recv.at[p, 0], {"cast": z + 1})

    def lo_arrives(p, r):
        hi_copy(p, r).wait_recv()

    def hi_arrives(p, r):
        lo_copy(p, r).wait_recv()

    loads[2].wait()

    def first_step(d, r):
        part = pl.ds(8 * r, 8)
        h = shell_out[d, part, :]
        u = thermal_map(h)
        UA[d + 1, part, :] = u
        if r == 0:
            edge_out[0, 0, pl.ds(d, 1), :] = u[0:1, :]
        if r == tiles - 1:
            edge_out[0, 1, pl.ds(d, 1), :] = u[7:8, :]

    for r in range(tiles):
        first_step(0, r)
        pl.when(has_lo)(lo_copy(0, r).start)
        first_step(depth - 1, r)
        pl.when(has_hi)(hi_copy(0, r).start)

    @pl.loop(1, depth - 1)
    def _(d):
        for r in range(tiles):
            first_step(d, r)

    pl.when(has_up)(up_copy(0).start)
    pl.when(has_down)(down_copy(0).start)

    col_left.wait_recv()
    col_right.wait_recv()
    corner_out[0] = col_in[:, 0:W, :]
    corner_out[1] = col_in[:, rows - W : rows, :]
    pl.when(has_up)(cor_up.start)
    pl.when(has_down)(cor_down.start)

    def unpack(l, before, after, lanes):
        after = pltpu.roll(after, (128 - W * l) % 128, axis=1)
        before = pltpu.roll(before, 128 - W - W * l, axis=1)
        zero = jnp.zeros_like(after)
        return jnp.where(lanes < W, after, jnp.where(lanes >= 128 - W, before, zero))

    for l in range(full):
        X[l, 0:rows, width : width + 128] = unpack(l, col_in[0], col_in[1], lane_r)
    corner_all[...] = jnp.zeros_like(corner_all)

    @pl.when(has_up)
    def _():
        row_down.wait_recv()
        cor_down.wait_recv()
        X[:, rows + 8 - W : rows + 8, 0:width] = row_in[0]
        corner_all[:, 8 - W : 8, :] = corner_in[0]

    @pl.when(has_down)
    def _():
        row_up.wait_recv()
        cor_up.wait_recv()
        X[:, rows : rows + W, 0:width] = row_in[1]
        corner_all[:, 0:W, :] = corner_in[1]

    for l in range(full):
        X[l, rows : rows + 8, width : width + 128] = unpack(
            l, corner_all[0], corner_all[1], lane_r[0:8]
        )

    row_id = lax.broadcasted_iota(jnp.int32, (rows + 8, width + 128), 0)
    at_top = (row_id == 0) & (z == 0)
    at_bottom = (row_id == rows - 1) & (z == m - 1)
    conduct = layers + 1

    def film_layer(l, below, first):
        film = X[l]
        above = X[l + 1]
        k = X[conduct]
        prev_row = jnp.where(at_top, film, pltpu.roll(film, 1, axis=0))
        next_row = jnp.where(at_bottom, film, pltpu.roll(film, rows + 7, axis=0))
        lateral = (
            prev_row
            + next_row
            + pltpu.roll(film, 1, axis=1)
            + pltpu.roll(film, width + 127, axis=1)
            - 4.0 * film
        )
        normal = normal_gain * k * (above + below - 2.0 * film)
        if first:
            normal = normal - X[layers + 2] * film
        X[l] = film + advance_flux_film * (k * lateral + normal)
        return film

    sub = lax.broadcasted_iota(jnp.int32, (8, perim), 0)

    def cell(p, q, d, r, below, above, heated, final):
        part = pl.ds(8 * r, 8)
        c = U[p][d + 1, part, :]
        if r == 0:
            edge = jnp.where(has_up, edge_in[p, 0, pl.ds(d, 1), :], c[0:1, :])
            prev_row = jnp.where(sub == 0, edge, pltpu.roll(c, 1, axis=0))
        else:
            prev_row = U[p][d + 1, pl.ds(8 * r - 1, 8), :]
        if r == tiles - 1:
            edge = jnp.where(has_down, edge_in[p, 1, pl.ds(d, 1), :], c[7:8, :])
            next_row = jnp.where(sub == 7, edge, pltpu.roll(c, 7, axis=0))
        else:
            next_row = U[p][d + 1, pl.ds(8 * r + 1, 8), :]
        lap = (
            U[p][below, part, :]
            + U[p][above, part, :]
            + prev_row
            + next_row
            + pltpu.roll(c, 1, axis=1)
            + pltpu.roll(c, perim - 1, axis=1)
            - 6.0 * c
        )
        h = shell_out[d, part, :] + shell_step * lap
        if heated:
            h = h + shell_step * heat[part, :]
        shell_out[d, part, :] = h
        if final and not heated:
            return
        u = thermal_map(h)
        U[q][d + 1, part, :] = u
        if final:
            return
        if r == 0:
            edge_out[q, 0, pl.ds(d, 1), :] = u[0:1, :]
        if r == tiles - 1:
            edge_out[q, 1, pl.ds(d, 1), :] = u[7:8, :]

    below_first = jnp.where(has_lo, 0, 1)
    above_last = jnp.where(has_hi, depth + 1, depth)

    def ends(p, r, later, final, early):
        q = 1 - p
        pl.when(has_lo & later)(lambda: lo_copy(q, r).wait_send())
        pl.when(has_hi & later)(lambda: hi_copy(q, r).wait_send())
        pl.when(has_lo)(lambda: lo_arrives(p, r))
        pl.when(has_hi)(lambda: hi_arrives(p, r))
        cell(p, q, 0, r, below_first, 2, not early, final)
        cell(p, q, depth - 1, r, depth - 1, above_last, False, final)
        if not final:
            pl.when(has_lo)(lambda: lo_copy(q, r).start())
            pl.when(has_hi)(lambda: hi_copy(q, r).start())

    def sweep(p, later, final, early=False):
        q = 1 - p
        outer, inner = (0, tiles - 1), range(1, tiles - 1)
        pl.when(has_up & later)(lambda: up_copy(q).wait_send())
        pl.when(has_down & later)(lambda: down_copy(q).wait_send())
        pl.when(has_up)(lambda: down_copy(p).wait_recv())
        pl.when(has_down)(lambda: up_copy(p).wait_recv())
        for r in outer:
            ends(p, r, later, final, early)

        @pl.loop(1, depth - 1)
        def _(d):
            for r in outer:
                cell(p, q, d, r, d, d + 2, False, final)

        if not final:
            ready = has_lo if early else has_lo | True
            pl.when(has_up & ready)(lambda: up_copy(q).start())
            pl.when(has_down & ready)(lambda: down_copy(q).start())
        for r in inner:
            ends(p, r, later, final, early)
        if final:

            @pl.when(b == 0)
            def _():
                for k in range(1, n):
                    face_copy(k).start()

        @pl.loop(1, depth - 1)
        def _(d):
            for r in inner:
                cell(p, q, d, r, d, d + 2, False, final)

    end = SHELL_SWEEPS % 2

    def face_copy(k):
        return remote(
            U[end].at[1, :, k * width : (k + 1) * width], face_in, face_send.at[k], face_recv, {"blk": k}
        )

    sweep(0, has_up & False, False, True)

    @pl.loop(0, FILM_SWEEPS)
    def _(step):
        under = film_layer(0, X[0], True)
        for l in range(1, layers):
            under = film_layer(l, under, False)

    flux = normal_gain * X[conduct, 0:rows, 0:width] * (
        X[layers - 1, 0:rows, 0:width] - X[layers, 0:rows, 0:width]
    )
    own = pl.ds(pl.multiple_of(b * width, width), width)
    to_root = remote(flux_out, heat.at[:, own], flux_send, flux_recv.at[b], {"blk": 0})

    @pl.when(has_lo)
    def _():
        flux_out[...] = flux
        to_root.start()
        heat[...] = jnp.zeros_like(heat)

    @pl.when(b == 0)
    def _():
        heat[:, 0:width] = flux

    film_out[...] = X[0:layers, 0:rows, 0:width]

    @pl.when(b == 0)
    def _():
        for k in range(1, n):
            remote(
                flux_out, heat.at[:, k * width : (k + 1) * width], flux_send, flux_recv.at[k], {"blk": 1}
            ).wait_recv()
        for r in range(tiles):
            part = pl.ds(8 * r, 8)
            h = shell_out[0, part, :] + shell_step * heat[part, :]
            shell_out[0, part, :] = h
            u = thermal_map(h)
            UB[1, part, :] = u
            if r == 0:
                edge_out[1, 0, 0:1, :] = u[0:1, :]
            if r == tiles - 1:
                edge_out[1, 1, 0:1, :] = u[7:8, :]
        pl.when(has_up)(lambda: up_copy(1).start())
        pl.when(has_down)(lambda: down_copy(1).start())

    pairs = (SHELL_SWEEPS - 2) // 2

    @pl.loop(0, pairs)
    def _(k):
        sweep(1, k >= 0, False)
        sweep(0, k >= 0, False)

    for step in range(2 * pairs + 1, SHELL_SWEEPS):
        sweep(step % 2, has_up | True, step == SHELL_SWEEPS - 1)

    @pl.when(b == 0)
    def _():
        surf_out[...] = U[end][1, :, 0:width]

    @pl.when(has_lo)
    def _():
        face_copy(1).wait_recv()
        surf_out[...] = face_in[...]

    @pl.when(b == 0)
    def _():
        for k in range(1, n):
            face_copy(k).wait_send()

    q = 1 - end
    col_left.wait_send()
    col_right.wait_send()

    @pl.when(has_up)
    def _():
        row_up.wait_send()
        cor_up.wait_send()
        up_copy(q).wait_send()

    @pl.when(has_down)
    def _():
        row_down.wait_send()
        cor_down.wait_send()
        down_copy(q).wait_send()

    @pl.when(has_lo)
    def _():
        to_root.wait_send()
        for r in range(tiles):
            lo_copy(q, r).wait_send()

    @pl.when(has_hi)
    def _():
        for r in range(tiles):
            hi_copy(q, r).wait_send()


def body(n, m, film_temp, surface_temp, shell_enthalpy, phase_codes, zone_ids, zone_htc):
    layers, rows, width = film_temp.shape
    depth, _, perim = shell_enthalpy.shape
    tiles = rows // 8
    full = layers + 3
    f32 = jnp.float32
    vmem = pl.BlockSpec(memory_space=pltpu.VMEM)
    hbm = pl.BlockSpec(memory_space=pl.ANY)
    smem = pl.BlockSpec(memory_space=pltpu.SMEM)
    dma = pltpu.SemaphoreType.DMA
    return pl.pallas_call(
        functools.partial(kernel, n, m),
        out_shape=[
            jax.ShapeDtypeStruct(film_temp.shape, f32),
            jax.ShapeDtypeStruct(shell_enthalpy.shape, f32),
            jax.ShapeDtypeStruct(surface_temp.shape, f32),
        ],
        in_specs=[hbm, hbm, hbm, smem, smem, smem],
        out_specs=[vmem, vmem, vmem],
        scratch_shapes=[
            pltpu.VMEM((full, rows + 8, width + 128), f32),
            pltpu.VMEM((2, rows, 128), f32),
            pltpu.VMEM((2, rows, 128), f32),
            pltpu.VMEM((2, full, W, width), f32),
            pltpu.VMEM((2, full, W, width), f32),
            pltpu.VMEM((2, 2, W, 128), f32),
            pltpu.VMEM((2, 2, W, 128), f32),
            pltpu.VMEM((2, 8, 128), f32),
            pltpu.VMEM((depth + 2, rows, perim), f32),
            pltpu.VMEM((depth + 2, rows, perim), f32),
            pltpu.VMEM((2, 2, depth, perim), f32),
            pltpu.VMEM((2, 2, depth, perim), f32),
            pltpu.VMEM((rows, perim), f32),
            pltpu.VMEM((rows, width), f32),
            pltpu.VMEM((rows, width), f32),
            dma((6,)),
            dma((6,)),
            dma(()),
            dma((n,)),
            dma((n,)),
            dma(()),
            dma((2, 2, tiles)),
            dma((2, 2, tiles)),
            dma((2, 2)),
            dma((2, 2)),
            dma((3,)),
        ],
        compiler_params=pltpu.CompilerParams(
            collective_id=0, has_side_effects=True, vmem_limit_bytes=60 * 1024 * 1024
        ),
    )(film_temp, surface_temp, shell_enthalpy, phase_codes, zone_ids, zone_htc)


def solution(mesh):
    placed = (
        P(None, "cast", "blk"),
        P("cast", "blk"),
        P("blk", "cast", None),
        P("cast", "blk"),
        P("cast"),
        P(),
    )
    return jax.shard_map(
        functools.partial(body, mesh.shape["blk"], mesh.shape["cast"]),
        mesh=mesh,
        in_specs=placed,
        out_specs=(P(None, "cast", "blk"), P("blk", "cast", None), P("cast", "blk")),
        check_vma=False,
    )
```
